768 devices in a mesh: ctx: 96 (over y_lo, z, core), head: 8 (over y_hi, x).
Axes of the slice: x: 4, y: 8 (y_hi: 2, y_lo: 4; y = y_hi * 4 + y_lo), z: 12, core: 2. Of those that a mesh axis runs over, the one named last changes fastest.
Arguments:
- queries: bfloat16 [24576, 5120], P('ctx', 'head'), may hold values from -6 to 6
- keys: bfloat16 [24576, 1024], P('ctx', 'head'), may hold values from -6 to 6
- values: bfloat16 [24576, 1024], P('ctx', 'head'), may hold values from -6 to 6
- segment_ids: int32 [24576], P('ctx'), may hold values from 0 to 191, never falling along the last dimension, each value on 1 to 1280 neighbouring positions
- out_weight: bfloat16 [5120, 5120], P('head'), may hold values from -0.078125 to 0.078125
Outputs:
- projected: bfloat16 [24576, 5120], P('ctx', 'head')
The draws below stay inside these ranges and needn't reach their ends.
Inputs may be any that keep to these rules, and one draw needn't show every extreme that they name: `segment_ids`: ids never fall along the tokens; each document holds 1 to 6 - 1 times 256 tokens, one exactly that many; every id of 0 to 191 is used.
All inputs are finite; a program needn't handle non-finite values.
Results may differ from the reference program's by a relative error of at most 0.019.
Values may be sent and summed in bfloat16 or wider, within the bound.
A program may use at most 32 MiB of HBM per device.

```python
import math
import jax
import jax.numpy as jnp
import numpy as np
from jax import lax

D = 5120
HEADS = 40
KV_HEADS = 8
HD = 128
TOK_DEV = 256
SPAN = 6
TOKENS = 24576
DOCS = 192
N_HEAD = 8


def draw_queries(key, part):
    key = jax.random.fold_in(key, 3)
    first = jax.random.fold_in(key, 0)
    field = jnp.clip(jax.random.normal(first, (TOKENS, HEADS, HD), jnp.float32), -6.0, 6.0)
    return field.reshape(TOKENS, HEADS * HD).astype(jnp.bfloat16)


def draw_keys(key, part):
    key = jax.random.fold_in(key, 5)
    first = jax.random.fold_in(key, 0)
    field = jnp.clip(jax.random.normal(first, (TOKENS, KV_HEADS, HD), jnp.float32), -6.0, 6.0)
    return field.reshape(TOKENS, KV_HEADS * HD).astype(jnp.bfloat16)


def steps_of(stream_key, dims, cuts, smallest, top_value):
    def one(position, parts):
        heights = jax.random.uniform(jax.random.fold_in(jax.random.fold_in(stream_key, 6), position), (parts,), jnp.float32, smallest / len(cuts), top_value / len(cuts))
        return jnp.repeat(jnp.exp(heights), dims[position] // parts).reshape((-1,) + (1,) * (len(dims) - position - 1))

    level = one(*cuts[0])
    for cut in cuts[1:]:
        level = level * one(*cut)
    return level


def length_profile(number_of, total, bound, skew):
    loads = [(1 << 20) // math.isqrt(rank ** skew) + 1 for rank in range(2, number_of + 1)]
    rest, given = total - bound - (number_of - 1), [1] * (number_of - 1)
    while rest > 0:
        candidates = [i for i in range(number_of - 1) if given[i] < bound]
        pool, remaining = sum([loads[i] for i in candidates]), rest
        for i in candidates:
            more = min(bound - given[i], max(1, remaining * loads[i] // pool), rest)
            given[i] = given[i] + more
            rest = rest - more
    return np.array([bound] + given)


def uneven_parts(rng, amount, total, bound, skew):
    if amount == 2:
        one = jax.random.randint(rng, (), max(1, total - bound), min(bound, total - 1) + 1)
        return jnp.stack([one, total - one])
    lengths = jnp.asarray(length_profile(amount, total, bound, skew), jnp.int32)
    couples = (amount - 1) // 2
    giver, sink = lengths[1:1 + 2 * couples:2], lengths[2:2 + 2 * couples:2]
    room = jnp.minimum(giver - 1, bound - sink)
    passed = jax.random.randint(jax.random.fold_in(rng, 1), (couples,), 0, 1 << 20) % (room + 1)
    lengths = lengths.at[1:1 + 2 * couples:2].set(giver - passed).at[2:2 + 2 * couples:2].set(sink + passed)
    return lengths[jax.random.permutation(jax.random.fold_in(rng, 2), amount)]


def bell_draw(own_key, extent, scale, bound, pieces=(), kind=jnp.bfloat16):
    loudness = steps_of(own_key, extent, pieces, -0.22, 0.18) if pieces else 1.0
    values = jax.random.normal(own_key, extent, jnp.float32) * scale * loudness
    return jnp.minimum(jnp.maximum(values, -bound), bound).astype(kind)


def setup_inputs(seed: int = 0) -> dict:
    seeds = jax.random.split(jax.random.key(seed), 6)
    return {
        "queries": draw_queries(jax.random.fold_in(seeds[5], 71), 0),
        "keys": draw_keys(jax.random.fold_in(seeds[5], 71), 0),
        "values": bell_draw(seeds[2], (TOKENS, KV_HEADS * HD), 1.0, 6.0, ((0, 96), (1, 8))),
        "segment_ids": jnp.searchsorted(jnp.cumsum(uneven_parts(seeds[3], DOCS, TOKENS, (SPAN - 1) * TOK_DEV, 2)), jnp.arange(TOKENS), side="right").astype(jnp.int32),
        "out_weight": bell_draw(seeds[4], (HEADS * HD, D), (HEADS * HD) ** -0.5, 0.078125, ((0, 8),)),
    }


def reference(queries, keys, values, segment_ids, out_weight):
    total_rows = queries.shape[0]
    width = HEADS * HD
    kv_width = KV_HEADS * HD
    sharing = HEADS // KV_HEADS
    back = (SPAN - 1) * TOK_DEV
    key_pad = jnp.concatenate([jnp.zeros((back, kv_width), jnp.bfloat16), keys], axis=0)
    val_pad = jnp.concatenate([jnp.zeros((back, kv_width), jnp.bfloat16), values], axis=0)
    seg_pad = jnp.concatenate([jnp.full((back,), -1, jnp.int32), segment_ids.astype(jnp.int32)], axis=0)
    scaling = 1.0 / (HD ** 0.5)

    def one_block(block):
        start = (block * TOK_DEV).astype(jnp.int32)
        query_rows = lax.dynamic_slice_in_dim(queries, start, TOK_DEV, 0).reshape(TOK_DEV, KV_HEADS, sharing, HD)
        query_seg = lax.dynamic_slice_in_dim(segment_ids.astype(jnp.int32), start, TOK_DEV, 0)
        key_rows = lax.dynamic_slice_in_dim(key_pad, start, SPAN * TOK_DEV, 0).reshape(SPAN * TOK_DEV, KV_HEADS, HD)
        val_rows = lax.dynamic_slice_in_dim(val_pad, start, SPAN * TOK_DEV, 0).reshape(SPAN * TOK_DEV, KV_HEADS, HD)
        key_seg = lax.dynamic_slice_in_dim(seg_pad, start, SPAN * TOK_DEV, 0)
        query_pos = start + jnp.arange(TOK_DEV, dtype=jnp.int32)
        key_pos = start - back + jnp.arange(SPAN * TOK_DEV, dtype=jnp.int32)
        allowed = (query_seg[:, None] == key_seg[None, :]) & (key_pos[None, :] <= query_pos[:, None])
        scores = jnp.einsum("qgrd,kgd->grqk", query_rows.astype(jnp.float32), key_rows.astype(jnp.float32)) * scaling
        scores = jnp.where(allowed[None, None], scores, -1e30)
        peak = jnp.max(scores, axis=-1, keepdims=True)
        expo = jnp.exp(scores - peak)
        total = jnp.sum(expo, axis=-1)
        weights = expo.astype(jnp.bfloat16)
        summed = jnp.einsum("grqk,kgd->grqd", weights.astype(jnp.float32), val_rows.astype(jnp.float32))
        attended = (summed / total[..., None]).astype(jnp.bfloat16)
        return jnp.transpose(attended, (2, 0, 1, 3)).reshape(TOK_DEV, width)

    blocks = lax.map(one_block, jnp.arange(total_rows // TOK_DEV, dtype=jnp.int32))
    attended = blocks.reshape(total_rows, width)
    group_width = width // N_HEAD
    result = jnp.zeros((total_rows, D), jnp.float32)
    for index in range(N_HEAD):
        partial_term = jnp.dot(attended[:, index * group_width:(index + 1) * group_width], out_weight[index * group_width:(index + 1) * group_width], preferred_element_type=jnp.float32)
        rounded = lax.optimization_barrier(partial_term.astype(jnp.bfloat16))
        result = result + rounded.astype(jnp.float32)
    return result.astype(jnp.bfloat16)
```

```python
import functools
import math

import jax
import jax.numpy as jnp
from jax import lax
from jax.experimental import pallas as pl
from jax.experimental.pallas import tpu as pltpu
from jax.sharding import PartitionSpec as P

HD = 128
SPAN = 6
ROWS = 256
SEGROWS = 16
NX = 4
HALF = ROWS // 2
SUB = 128
NSUB = 5
MESH = pl.DeviceIdType.MESH
NEG = -1e30


def kernel(
    chips, share,
    q_hbm, k_hbm, v_hbm, s_hbm, w_hbm, out,
    q_v, kx, vv, seg_v, w_v, acc, att,
    s1, r1, keep, s2, r2, s3, r3,
    load_sem, ks_sem, kr_sem, vs_sem, vr_sem, fs_sem, fr_sem,
):
    ctx = lax.axis_index("ctx")
    head = lax.axis_index("head")
    chip, core = ctx // 2, ctx % 2
    yh, x = head // NX, head % NX
    x1 = x + 1 - 2 * (x % 2)
    x3 = NX - 1 - x
    xo = (x + 2) % NX
    nxt, prv = (chip + 1) % chips, (chip + chips - 1) % chips
    dev_x1 = (ctx, yh * NX + x1)
    dev_x3 = (ctx, yh * NX + x3)
    dev_y = (ctx, (1 - yh) * NX + x)
    dev_sib = (chip * 2 + 1 - core, head)
    dev_next = (nxt * 2 + core, head)

    barrier = pltpu.get_barrier_semaphore()
    for device in (dev_y, dev_x1, dev_x3, dev_sib, (prv * 2 + core, head)):
        pl.semaphore_signal(barrier, inc=1, device_id=device, device_id_type=MESH)

    @pl.when(core == 0)
    def _():
        pl.semaphore_signal(barrier, inc=1, device_id=(prv * 2 + 1, head), device_id_type=MESH)

    loads = [
        pltpu.make_async_copy(s_hbm, seg_v, load_sem.at[0]),
        pltpu.make_async_copy(k_hbm, kx.at[0, pl.ds(0, ROWS)], load_sem.at[1]),
        pltpu.make_async_copy(v_hbm, vv.at[0], load_sem.at[2]),
        pltpu.make_async_copy(q_hbm, q_v, load_sem.at[3]),
        pltpu.make_async_copy(w_hbm, w_v, load_sem.at[4]),
    ]
    for load in loads:
        load.start()

    for d in range(1, SPAN):
        @pl.when(ctx < d)
        def _():
            kx[d, 0:ROWS, :] = jnp.zeros((ROWS, HD), jnp.bfloat16)
            kx[d, ROWS:, :] = jnp.full((SEGROWS, HD), -1.0, jnp.bfloat16)
            vv[d] = jnp.zeros((ROWS, HD), jnp.bfloat16)

    loads[0].wait()
    seg = seg_v[...].astype(jnp.float32)
    seg_lo, seg_hi = seg[:, :HD], seg[:, HD:]
    line = lax.broadcasted_iota(jnp.int32, (SEGROWS, HD), 0)
    both = jnp.where(line == 0, jnp.broadcast_to(seg_lo, (SEGROWS, HD)), jnp.broadcast_to(seg_hi, (SEGROWS, HD)))
    kx[0, ROWS:, :] = both.astype(jnp.bfloat16)
    first = jnp.min(seg, axis=1, keepdims=True)
    loads[1].wait()
    loads[2].wait()
    pl.semaphore_wait(barrier, 5 + core)

    def k_copy(index, slot, to_slot, device):
        return pltpu.make_async_remote_copy(
            src_ref=kx.at[slot], dst_ref=kx.at[to_slot],
            send_sem=ks_sem.at[index], recv_sem=kr_sem.at[to_slot],
            device_id=device, device_id_type=MESH)

    def v_copy(index, slot, to_slot, device):
        return pltpu.make_async_remote_copy(
            src_ref=vv.at[slot], dst_ref=vv.at[to_slot],
            send_sem=vs_sem.at[index], recv_sem=vr_sem.at[to_slot],
            device_id=device, device_id_type=MESH)

    plan = [
        (0, 2, dev_next, chip < chips - 1),
        (0, 1, dev_sib, core == 0),
        (2, 4, dev_next, (chip >= 1) & (chip < chips - 1)),
        (2, 3 - 2 * core, dev_sib, chip >= 1),
        (4, 5, (nxt * 2, head), (chip >= 2) & (chip < chips - 1) & (core == 1)),
        (4, 5 - 2 * core, dev_sib, chip >= 2),
    ]

    def send(make, slot):
        for index, (source, target, device, cond) in enumerate(plan):
            if source == slot:
                @pl.when(cond)
                def _():
                    make(index, source, target, device).start()

    def arrive(make, slot):
        @pl.when(ctx >= slot)
        def _():
            make(0, slot, slot, dev_next).wait_recv()

    send(k_copy, 0)
    send(v_copy, 0)
    loads[3].wait()

    scale = math.log2(math.e) / math.sqrt(HD)
    key_row = lax.broadcasted_iota(jnp.int32, (ROWS, ROWS), 0)
    peaks, totals = [None] * share, [None] * share

    def absorb(slot, allowed):
        vt = vv[slot].T
        for h in range(share):
            scores = lax.dot_general(
                kx[slot, 0:ROWS, :], q_v[:, h * HD:(h + 1) * HD],
                (((1,), (1,)), ((), ())), preferred_element_type=jnp.float32)
            scores = jnp.where(allowed, scores, NEG)
            top = jnp.max(scores, axis=0, keepdims=True)
            if slot > 0:
                top = jnp.maximum(top, peaks[h])
            expo = jnp.exp2((scores - top) * scale)
            total = jnp.sum(expo, axis=0, keepdims=True)
            part = jnp.dot(vt, expo.astype(jnp.bfloat16), preferred_element_type=jnp.float32)
            if slot > 0:
                factor = jnp.exp2((peaks[h] - top) * scale)
                total = total + totals[h] * factor
                part = part + acc[h] * factor
            peaks[h], totals[h] = top, total
            if slot < SPAN - 1:
                acc[h] = part
            else:
                att[:, h * HD:(h + 1) * HD] = (part / total).T.astype(jnp.bfloat16)

    seg_col = jnp.concatenate(
        [jnp.broadcast_to(seg_lo, (HD, HD)).T, jnp.broadcast_to(seg_hi, (HD, HD)).T], axis=0)
    seg_col = jnp.concatenate([seg_col, seg_col], axis=1)
    query_col = lax.broadcasted_iota(jnp.int32, (ROWS, ROWS), 1)
    absorb(0, (seg_col == seg) & (key_row <= query_col))
    for slot in (2, 1, 4, 3, 5):
        arrive(k_copy, slot)
        send(k_copy, slot)
        arrive(v_copy, slot)
        send(v_copy, slot)
        ids = kx[slot, ROWS:, :].astype(jnp.float32)
        same = jnp.where((line < 2) & (ids == first), 1.0, 0.0)
        count = jnp.sum(jnp.sum(same, axis=0, keepdims=True), axis=1, keepdims=True)
        start = jnp.where(seg == first, ROWS - count, float(ROWS)).astype(jnp.int32)
        absorb(slot, key_row >= start)

    loads[4].wait()

    pairs = ((dev_x1, dev_x3), (dev_x3, dev_x1))

    def column(xx, yi, j):
        yy = yh if yi == 0 else 1 - yh
        return pl.ds(pl.multiple_of((yy * NX + xx) * (SUB * NSUB) + j * SUB, SUB), SUB)

    def product(xs, j):
        weights = jnp.concatenate([w_v[:, column(xx, yi, j)] for xx in xs for yi in range(2)], axis=1)
        return jnp.dot(att[...], weights, preferred_element_type=jnp.float32)

    def s1_copy(j, side):
        return pltpu.make_async_remote_copy(
            src_ref=s1.at[j, side], dst_ref=r1.at[j, side],
            send_sem=fs_sem.at[0, j, side], recv_sem=fr_sem.at[0, j, side],
            device_id=pairs[side][0], device_id_type=MESH)

    def s2_copy(j, side):
        return pltpu.make_async_remote_copy(
            src_ref=s2.at[j, side], dst_ref=r2.at[j, side],
            send_sem=fs_sem.at[1, j, side], recv_sem=fr_sem.at[1, j, side],
            device_id=pairs[side][1], device_id_type=MESH)

    def s3_copy(j, side):
        return pltpu.make_async_remote_copy(
            src_ref=s3.at[j, side], dst_ref=r3.at[j, side],
            send_sem=fs_sem.at[2, j, side], recv_sem=fr_sem.at[2, j, side],
            device_id=dev_y, device_id_type=MESH)

    def stage1(j):
        p = product((x1, xo), j)
        for b in range(4):
            piece = p[:, b * SUB:(b + 1) * SUB]
            s1[j, 0, b] = piece[:HALF].astype(jnp.bfloat16)
            if b < 2:
                keep[j, 1, 2 + b] = piece[HALF:]
            else:
                s1[j, 1, b] = piece[HALF:].astype(jnp.bfloat16)
        s1_copy(j, 0).start()
        p = product((x3, x), j)
        for b in range(4):
            piece = p[:, b * SUB:(b + 1) * SUB]
            if b < 2:
                s1[j, 1, b] = piece[HALF:].astype(jnp.bfloat16)
                keep[j, 0, 2 + b] = piece[:HALF]
            else:
                keep[j, 0, b - 2] = piece[:HALF]
                keep[j, 1, b - 2] = piece[HALF:]
        s1_copy(j, 1).start()

    def stage2(j):
        for side in range(2):
            s1_copy(j, side).wait_recv()
            for b in range(2):
                s2[j, side, b] = (keep[j, side, 2 + b] + r1[j, side, 2 + b].astype(jnp.float32)).astype(jnp.bfloat16)
            s2_copy(j, side).start()
            for b in range(2):
                keep[j, side, b] = keep[j, side, b] + r1[j, side, b].astype(jnp.float32)

    def stage3(j):
        for side in range(2):
            s2_copy(j, side).wait_recv()
            s3[j, side] = (keep[j, side, 1] + r2[j, side, 1].astype(jnp.float32)).astype(jnp.bfloat16)
            s3_copy(j, side).start()
            keep[j, side, 0] = keep[j, side, 0] + r2[j, side, 0].astype(jnp.float32)

    def finish(j):
        for side in range(2):
            s3_copy(j, side).wait_recv()
            out[side * HALF:(side + 1) * HALF, j * SUB:(j + 1) * SUB] = (
                keep[j, side, 0] + r3[j, side].astype(jnp.float32)).astype(jnp.bfloat16)

    stage1(0)
    stage1(1)
    for j in range(NSUB):
        stage2(j)
        if j + 2 < NSUB:
            stage1(j + 2)
        if j >= 1:
            stage3(j - 1)
        if j >= 3:
            finish(j - 3)
    stage3(NSUB - 1)
    for j in range(NSUB - 3, NSUB):
        finish(j)

    for j in range(NSUB):
        for side in range(2):
            s1_copy(j, side).wait_send()
            s2_copy(j, side).wait_send()
            s3_copy(j, side).wait_send()
    for make in (k_copy, v_copy):
        for index, (source, target, device, cond) in enumerate(plan):
            @pl.when(cond)
            def _():
                make(index, source, target, device).wait_send()


def solution(mesh):
    chips = mesh.shape["ctx"] // 2

    def shards(queries, keys, values, segment_ids, out_weight):
        share = queries.shape[1] // HD
        cols = out_weight.shape[1] // mesh.shape["head"]
        bf, f32 = jnp.bfloat16, jnp.float32
        return pl.pallas_call(
            functools.partial(kernel, chips, share),
            name="attend_project",
            out_shape=jax.ShapeDtypeStruct((ROWS, cols), bf),
            in_specs=[pl.BlockSpec(memory_space=pl.ANY)] * 5,
            out_specs=pl.BlockSpec(memory_space=pltpu.VMEM),
            scratch_shapes=[
                pltpu.VMEM(queries.shape, bf),
                pltpu.VMEM((SPAN, ROWS + SEGROWS, HD), bf),
                pltpu.VMEM((SPAN, ROWS, HD), bf),
                pltpu.VMEM((1, ROWS), jnp.int32),
                pltpu.VMEM(out_weight.shape, bf),
                pltpu.VMEM((share, HD, ROWS), f32),
                pltpu.VMEM(queries.shape, bf),
                pltpu.VMEM((NSUB, 2, 4, HALF, SUB), bf),
                pltpu.VMEM((NSUB, 2, 4, HALF, SUB), bf),
                pltpu.VMEM((NSUB, 2, 4, HALF, SUB), f32),
                pltpu.VMEM((NSUB, 2, 2, HALF, SUB), bf),
                pltpu.VMEM((NSUB, 2, 2, HALF, SUB), bf),
                pltpu.VMEM((NSUB, 2, HALF, SUB), bf),
                pltpu.VMEM((NSUB, 2, HALF, SUB), bf),
                pltpu.SemaphoreType.DMA((5,)),
                pltpu.SemaphoreType.DMA((SPAN,)),
                pltpu.SemaphoreType.DMA((SPAN,)),
                pltpu.SemaphoreType.DMA((SPAN,)),
                pltpu.SemaphoreType.DMA((SPAN,)),
                pltpu.SemaphoreType.DMA((3, NSUB, 2)),
                pltpu.SemaphoreType.DMA((3, NSUB, 2)),
            ],
            compiler_params=pltpu.CompilerParams(
                collective_id=0, has_side_effects=True, vmem_limit_bytes=60 * 2**20),
        )(queries, keys, values, segment_ids.reshape(1, ROWS), out_weight)

    in_specs = (P("ctx", "head"), P("ctx", "head"), P("ctx", "head"), P("ctx"), P("head", None))
    return jax.shard_map(shards, mesh=mesh, in_specs=in_specs, out_specs=P("ctx", "head"), check_vma=False)
```

```python
import functools
import math

import jax
import jax.numpy as jnp
from jax import lax
from jax.experimental import pallas as pl
from jax.experimental.pallas import tpu as pltpu
from jax.sharding import PartitionSpec as P

HD = 128
SPAN = 6
ROWS = 256
SEGROWS = 16
NX = 4
NZ = 12
BLOCK = 640
PARTS = (((0, 384, 0), (0, 256, 384)), ((384, 256, 0), (256, 384, 256)))
CHUNKS = ((0, 64), (64, 64), (128, 64), (192, 64))
NCH = len(CHUNKS)
MESH = pl.DeviceIdType.MESH
NEG = -1e30
LANES = 128


def kernel(
    chips, share,
    q_hbm, k_hbm, v_hbm, s_hbm, w_hbm, out,
    q_v, kx, vv, seg_v, wx, acc, att, attx, own, s2, r2, res, s3, r3,
    load_sem, ks_sem, kr_sem, vs_sem, vr_sem, ws_sem, wr_sem, as_sem, ar_sem, fs_sem, fr_sem,
):
    ctx = lax.axis_index("ctx")
    head = lax.axis_index("head")
    chip, core = ctx // 2, ctx % 2
    yh, x = head // NX, head % NX
    x1 = x + 1 - 2 * (x % 2)
    x3 = NX - 1 - x
    xo = (x + 2) % NX
    nxt, prv = (chip + 1) % chips, (chip + chips - 1) % chips
    dev_x1 = (ctx, yh * NX + x1)
    dev_x3 = (ctx, yh * NX + x3)
    dev_y = (ctx, (1 - yh) * NX + x)
    dev_sib = (chip * 2 + 1 - core, head)
    dev_next = (nxt * 2 + core, head)

    barrier = pltpu.get_barrier_semaphore()
    for device in (dev_y, dev_x1, dev_x3, dev_sib, (prv * 2 + core, head)):
        pl.semaphore_signal(barrier, inc=1, device_id=device, device_id_type=MESH)

    @pl.when(core == 0)
    def _():
        pl.semaphore_signal(barrier, inc=1, device_id=(prv * 2 + 1, head), device_id_type=MESH)

    depth = w_hbm.shape[0]
    dests = ((x, x3), (x, x1))
    partner = ((dev_x1, x1, xo), (dev_x3, x3, xo))

    def span(xx, yy, side):
        first, width, _ = PARTS[side][yy]
        return pl.ds(pl.multiple_of((yy * NX + xx) * BLOCK + first, HD), width)

    def spot(d, yy, side):
        return pl.ds(d * BLOCK + PARTS[side][yy][2], PARTS[side][yy][1])

    part = depth // 2
    mine = pl.ds(pl.multiple_of(core * part, 16), part)
    theirs = pl.ds(pl.multiple_of(depth + core * part, 16), part)
    others = pl.ds(pl.multiple_of(depth + (1 - core) * part, 16), part)
    loads = [
        pltpu.make_async_copy(s_hbm, seg_v, load_sem.at[0]),
        pltpu.make_async_copy(k_hbm, kx.at[0, pl.ds(0, ROWS)], load_sem.at[1]),
        pltpu.make_async_copy(v_hbm, vv.at[0], load_sem.at[2]),
        pltpu.make_async_copy(q_hbm, q_v, load_sem.at[3]),
    ]
    w_sends = []
    for side in range(2):
        for d in range(2):
            for yy in range(2):
                n = (side * 2 + d) * 2 + yy
                loads.append(pltpu.make_async_copy(
                    w_hbm.at[:, span(dests[side][d], yy, side)],
                    wx.at[side, pl.ds(0, depth), spot(d, yy, side)], load_sem.at[4 + n]))
                device, *columns = partner[side]
                w_sends.append(pltpu.make_async_remote_copy(
                    src_ref=w_hbm.at[mine, span(columns[d], yy, side)],
                    dst_ref=wx.at[side, theirs, spot(d, yy, side)],
                    send_sem=ws_sem.at[n], recv_sem=wr_sem.at[n],
                    device_id=device, device_id_type=MESH))

    def w_copy(n, rows):
        side, d, yy = n // 4, n // 2 % 2, n % 2
        block = wx.at[side, rows, spot(d, yy, side)]
        return pltpu.make_async_remote_copy(
            src_ref=block, dst_ref=block, send_sem=ws_sem.at[8 + n], recv_sem=wr_sem.at[8 + n],
            device_id=dev_sib, device_id_type=MESH)

    def pass_weights():
        for n in (0, 4, 1, 5, 2, 6, 3, 7):
            w_sends[n].wait_recv()
            w_copy(n, theirs).start()

    for load in loads:
        load.start()

    for d in range(1, SPAN):
        @pl.when(ctx < d)
        def _():
            kx[d, 0:ROWS, :] = jnp.zeros((ROWS, HD), jnp.bfloat16)
            kx[d, ROWS:, :] = jnp.full((SEGROWS, HD), -1.0, jnp.bfloat16)
            vv[d] = jnp.zeros((ROWS, HD), jnp.bfloat16)

    loads[0].wait()
    seg = seg_v[...].astype(jnp.float32)
    seg_lo, seg_hi = seg[:, :HD], seg[:, HD:]
    line = lax.broadcasted_iota(jnp.int32, (SEGROWS, HD), 0)
    both = jnp.where(line == 0, jnp.broadcast_to(seg_lo, (SEGROWS, HD)), jnp.broadcast_to(seg_hi, (SEGROWS, HD)))
    kx[0, ROWS:, :] = both.astype(jnp.bfloat16)
    first = jnp.min(seg, axis=1, keepdims=True)
    loads[1].wait()
    loads[2].wait()
    pl.semaphore_wait(barrier, 5 + core)

    def k_copy(index, slot, to_slot, device):
        return pltpu.make_async_remote_copy(
            src_ref=kx.at[slot], dst_ref=kx.at[to_slot],
            send_sem=ks_sem.at[index], recv_sem=kr_sem.at[to_slot],
            device_id=device, device_id_type=MESH)

    def v_copy(index, slot, to_slot, device):
        return pltpu.make_async_remote_copy(
            src_ref=vv.at[slot], dst_ref=vv.at[to_slot],
            send_sem=vs_sem.at[index], recv_sem=vr_sem.at[to_slot],
            device_id=device, device_id_type=MESH)

    plan = [
        (0, 2, dev_next, chip < chips - 1),
        (0, 1, dev_sib, core == 0),
        (2, 4, dev_next, (chip >= 1) & (chip < chips - 1)),
        (2, 3 - 2 * core, dev_sib, chip >= 1),
        (4, 5, (nxt * 2, head), (chip >= 2) & (chip < chips - 1) & (core == 1)),
        (4, 5 - 2 * core, dev_sib, chip >= 2),
    ]

    def send(make, slot, extra=True):
        for index, (source, target, device, cond) in enumerate(plan):
            if source == slot:
                @pl.when(cond & extra)
                def _():
                    make(index, source, target, device).start()

    def arrive(make, slot):
        @pl.when(ctx >= slot)
        def _():
            make(0, slot, slot, dev_next).wait_recv()

    send(k_copy, 0)
    send(v_copy, 0)
    for n in (0, 4, 1, 5, 2, 6, 3, 7):
        w_sends[n].start()
    loads[3].wait()

    scale = math.log2(math.e) / math.sqrt(HD)
    key_row = lax.broadcasted_iota(jnp.int32, (ROWS, ROWS), 0)
    count = share * (ROWS // LANES)
    peaks, totals = [None] * count, [None] * count

    def a_copy(side, n, rows, columns):
        return pltpu.make_async_remote_copy(
            src_ref=att.at[rows, columns], dst_ref=attx.at[side, rows, columns],
            send_sem=as_sem.at[side, n], recv_sem=ar_sem.at[side, n],
            device_id=partner[side][0], device_id_type=MESH)

    def a_copies(side, r):
        rows = pl.ds(*CHUNKS[r])
        if r == 0:
            return [a_copy(side, h, rows, pl.ds(h * HD, HD)) for h in range(share)]
        return [a_copy(side, share + r - 1, rows, pl.ds(0, share * HD))]

    def absorb(slot, allowed, place):
        vt = vv[slot].T
        for h in range(share):
            for half in range(ROWS // LANES):
                cols = slice(half * LANES, (half + 1) * LANES)
                n = h * (ROWS // LANES) + half
                scores = lax.dot_general(
                    kx[slot, 0:ROWS, :], q_v[cols, h * HD:(h + 1) * HD],
                    (((1,), (1,)), ((), ())), preferred_element_type=jnp.float32)
                scores = jnp.where(allowed[:, cols], scores, NEG)
                top = jnp.max(scores, axis=0, keepdims=True)
                if place > 0:
                    top = jnp.maximum(top, peaks[n])
                expo = jnp.exp2((scores - top) * scale)
                total = jnp.sum(expo, axis=0, keepdims=True)
                part = jnp.dot(vt, expo.astype(jnp.bfloat16), preferred_element_type=jnp.float32)
                if place > 0:
                    factor = jnp.exp2((peaks[n] - top) * scale)
                    total = total + totals[n] * factor
                    part = part + acc[h, :, cols] * factor
                peaks[n], totals[n] = top, total
                if place < SPAN - 1:
                    acc[h, :, cols] = part
                else:
                    att[cols, h * HD:(h + 1) * HD] = (part / total).T.astype(jnp.bfloat16)
            if place == SPAN - 1:
                for side in range(2):
                    a_copy(side, h, pl.ds(*CHUNKS[0]), pl.ds(h * HD, HD)).start()

    seg_col = jnp.concatenate(
        [jnp.broadcast_to(seg_lo, (HD, HD)).T, jnp.broadcast_to(seg_hi, (HD, HD)).T], axis=0)
    seg_col = jnp.concatenate([seg_col, seg_col], axis=1)
    query_col = lax.broadcasted_iota(jnp.int32, (ROWS, ROWS), 1)
    absorb(0, (seg_col == seg) & (key_row <= query_col), 0)
    order = ((2 - core, core == 0), (1 + core, core == 1), (4 - core, core == 0), (3 + core, core == 1), (5, None))
    for place, (slot, passes) in enumerate(order):
        source = (2, 2, 4, 4, 5)[place]
        for make in (k_copy, v_copy):
            arrive(make, slot)
            if passes is not None:
                send(make, source, passes)
        ids = kx[slot, ROWS:, :].astype(jnp.float32)
        same = jnp.where((line < 2) & (ids == first), 1.0, 0.0)
        count = jnp.sum(jnp.sum(same, axis=0, keepdims=True), axis=1, keepdims=True)
        start = jnp.where(seg == first, ROWS - count, float(ROWS)).astype(jnp.int32)
        absorb(slot, key_row >= start, place + 1)
        if place == 3:
            pl.when(chip % NZ < 2)(pass_weights)

    def exchange(r):
        for side in range(2):
            for copy in a_copies(side, r):
                copy.start()

    exchange(1)
    for load in loads[4:]:
        load.wait()
    pl.when(chip % NZ >= 2)(pass_weights)

    def s2_copy(side, r):
        rows = pl.ds(*CHUNKS[r])
        return pltpu.make_async_remote_copy(
            src_ref=s2.at[side, rows], dst_ref=r2.at[side, rows],
            send_sem=fs_sem.at[side, r], recv_sem=fr_sem.at[side, r],
            device_id=partner[1 - side][0], device_id_type=MESH)

    def s3_copy(r):
        rows = pl.ds(*CHUNKS[r])
        return pltpu.make_async_remote_copy(
            src_ref=s3.at[1 - yh, rows], dst_ref=r3.at[rows],
            send_sem=fs_sem.at[2, r], recv_sem=fr_sem.at[2, r],
            device_id=dev_y, device_id_type=MESH)

    def rows_of(r):
        return slice(CHUNKS[r][0], CHUNKS[r][0] + CHUNKS[r][1])

    def own_part(r):
        for side in range(2):
            own[side, rows_of(r)] = jnp.dot(
                att[rows_of(r)], wx[side, 0:depth], preferred_element_type=jnp.float32)

    def both_parts(r):
        for side in range(2):
            for copy in a_copies(side, r):
                copy.wait_recv()
            if r == 0:
                for n in range(side * 4, side * 4 + 4):
                    w_copy(n, others).wait_recv()
            both = own[side, rows_of(r)] + jnp.dot(
                attx[side, rows_of(r)], wx[side, depth:], preferred_element_type=jnp.float32)
            s2[side, rows_of(r)] = both[:, BLOCK:].astype(jnp.bfloat16)
            s2_copy(side, r).start()
            own[side, rows_of(r), 0:BLOCK] = both[:, :BLOCK]

    def hand_on(r):
        for side in range(2):
            s2_copy(side, r).wait_recv()
            both = own[side, rows_of(r), 0:BLOCK] + r2[side, rows_of(r)].astype(jnp.float32)
            for yy in range(2):
                first, width, place = PARTS[side][yy]
                res[yy, rows_of(r), first:first + width] = both[:, place:place + width]
                s3[yy, rows_of(r), first:first + width] = both[:, place:place + width].astype(jnp.bfloat16)
        s3_copy(r).start()

    own_part(0)
    for r in range(NCH):
        both_parts(r)
        if r + 2 < NCH:
            exchange(r + 2)
        if r + 1 < NCH:
            own_part(r + 1)
        if r >= 1:
            hand_on(r - 1)
    hand_on(NCH - 1)

    for r in range(NCH):
        s3_copy(r).wait_recv()
        out[rows_of(r)] = (res[yh, rows_of(r)] + r3[rows_of(r)].astype(jnp.float32)).astype(jnp.bfloat16)
    for r in range(NCH):
        s3_copy(r).wait_send()
        for side in range(2):
            s2_copy(side, r).wait_send()
            for copy in a_copies(side, r):
                copy.wait_send()
    for copy in w_sends:
        copy.wait_send()
    for n in range(8):
        w_copy(n, theirs).wait_send()
    for make in (k_copy, v_copy):
        for index, (source, target, device, cond) in enumerate(plan):
            @pl.when(cond)
            def _():
                make(index, source, target, device).wait_send()


def solution(mesh):
    chips = mesh.shape["ctx"] // 2

    def shards(queries, keys, values, segment_ids, out_weight):
        share = queries.shape[1] // HD
        cols = out_weight.shape[1] // mesh.shape["head"]
        bf, f32 = jnp.bfloat16, jnp.float32
        depth = out_weight.shape[0]
        return pl.pallas_call(
            functools.partial(kernel, chips, share),
            name="attend_project",
            out_shape=pltpu.VMEM((ROWS, cols), bf),
            in_specs=[pl.BlockSpec(memory_space=pl.ANY)] * 5,
            out_specs=pl.BlockSpec(memory_space=pltpu.VMEM),
            scratch_shapes=[
                pltpu.VMEM(queries.shape, bf),
                pltpu.VMEM((SPAN, ROWS + SEGROWS, HD), bf),
                pltpu.VMEM((SPAN, ROWS, HD), bf),
                pltpu.VMEM((1, ROWS), jnp.int32),
                pltpu.VMEM((2, 2 * depth, 2 * BLOCK), bf),
                pltpu.VMEM((share, HD, ROWS), f32),
                pltpu.VMEM(queries.shape, bf),
                pltpu.VMEM((2, *queries.shape), bf),
                pltpu.VMEM((2, ROWS, 2 * BLOCK), f32),
                pltpu.VMEM((2, ROWS, BLOCK), bf),
                pltpu.VMEM((2, ROWS, BLOCK), bf),
                pltpu.VMEM((2, ROWS, BLOCK), f32),
                pltpu.VMEM((2, ROWS, BLOCK), bf),
                pltpu.VMEM((ROWS, BLOCK), bf),
                pltpu.SemaphoreType.DMA((12,)),
                pltpu.SemaphoreType.DMA((SPAN,)),
                pltpu.SemaphoreType.DMA((SPAN,)),
                pltpu.SemaphoreType.DMA((SPAN,)),
                pltpu.SemaphoreType.DMA((SPAN,)),
                pltpu.SemaphoreType.DMA((16,)),
                pltpu.SemaphoreType.DMA((16,)),
                pltpu.SemaphoreType.DMA((2, share + NCH - 1)),
                pltpu.SemaphoreType.DMA((2, share + NCH - 1)),
                pltpu.SemaphoreType.DMA((3, NCH)),
                pltpu.SemaphoreType.DMA((3, NCH)),
            ],
            compiler_params=pltpu.CompilerParams(
                collective_id=0, has_side_effects=True, vmem_limit_bytes=60 * 2**20),
        )(queries, keys, values, segment_ids.reshape(1, ROWS), out_weight)

    in_specs = (P("ctx", "head"), P("ctx", "head"), P("ctx", "head"), P("ctx"), P("head", None))
    return jax.shard_map(shards, mesh=mesh, in_specs=in_specs, out_specs=P("ctx", "head"), check_vma=False)
```

```python
import functools
import math

import jax
import jax.numpy as jnp
from jax import lax
from jax.experimental import pallas as pl
from jax.experimental.pallas import tpu as pltpu
from jax.sharding import PartitionSpec as P

HD = 128
SPAN = 6
ROWS = 256
SEGROWS = 16
NX = 4
NZ = 12
BLOCK = 640
PARTS = (((0, 384, 0), (0, 256, 384)), ((384, 256, 0), (256, 384, 256)))
CHUNKS = ((0, 64), (64, 64), (128, 64), (192, 64))
NCH = len(CHUNKS)
MESH = pl.DeviceIdType.MESH
NEG = -1e30
LANES = 128


def kernel(
    chips, share,
    q_hbm, k_hbm, v_hbm, s_hbm, w_hbm, out,
    q_v, kx, vv, seg_v, wx, acc, probs, att, attx, own, s2, r2, res, s3, r3,
    load_sem, ks_sem, kr_sem, vs_sem, vr_sem, ws_sem, wr_sem, as_sem, ar_sem, fs_sem, fr_sem,
):
    ctx = lax.axis_index("ctx")
    head = lax.axis_index("head")
    chip, core = ctx // 2, ctx % 2
    yh, x = head // NX, head % NX
    x1 = x + 1 - 2 * (x % 2)
    x3 = NX - 1 - x
    xo = (x + 2) % NX
    nxt, prv = (chip + 1) % chips, (chip + chips - 1) % chips
    dev_x1 = (ctx, yh * NX + x1)
    dev_x3 = (ctx, yh * NX + x3)
    dev_y = (ctx, (1 - yh) * NX + x)
    dev_sib = (chip * 2 + 1 - core, head)
    dev_next = (nxt * 2 + core, head)

    barrier = pltpu.get_barrier_semaphore()
    for device in (dev_y, dev_x1, dev_x3, dev_sib, (prv * 2 + core, head)):
        pl.semaphore_signal(barrier, inc=1, device_id=device, device_id_type=MESH)

    @pl.when(core == 0)
    def _():
        pl.semaphore_signal(barrier, inc=1, device_id=(prv * 2 + 1, head), device_id_type=MESH)

    depth = w_hbm.shape[0]
    dests = ((x, x3), (x, x1))
    partner = ((dev_x1, x1, xo), (dev_x3, x3, xo))

    def span(xx, yy, side):
        first, width, _ = PARTS[side][yy]
        return pl.ds(pl.multiple_of((yy * NX + xx) * BLOCK + first, HD), width)

    def spot(d, yy, side):
        return pl.ds(d * BLOCK + PARTS[side][yy][2], PARTS[side][yy][1])

    part = depth // 2
    mine = pl.ds(pl.multiple_of(core * part, 16), part)
    theirs = pl.ds(pl.multiple_of(depth + core * part, 16), part)
    others = pl.ds(pl.multiple_of(depth + (1 - core) * part, 16), part)
    loads = [
        pltpu.make_async_copy(s_hbm, seg_v, load_sem.at[0]),
        pltpu.make_async_copy(k_hbm, kx.at[0, pl.ds(0, ROWS)], load_sem.at[1]),
        pltpu.make_async_copy(v_hbm, vv.at[0], load_sem.at[2]),
        pltpu.make_async_copy(q_hbm, q_v, load_sem.at[3]),
    ]
    w_sends = []
    for side in range(2):
        for d in range(2):
            for yy in range(2):
                n = (side * 2 + d) * 2 + yy
                loads.append(pltpu.make_async_copy(
                    w_hbm.at[:, span(dests[side][d], yy, side)],
                    wx.at[side, pl.ds(0, depth), spot(d, yy, side)], load_sem.at[4 + n]))
                device, *columns = partner[side]
                w_sends.append(pltpu.make_async_remote_copy(
                    src_ref=w_hbm.at[mine, span(columns[d], yy, side)],
                    dst_ref=wx.at[side, theirs, spot(d, yy, side)],
                    send_sem=ws_sem.at[n], recv_sem=wr_sem.at[n],
                    device_id=device, device_id_type=MESH))

    def w_copy(n, rows):
        side, d, yy = n // 4, n // 2 % 2, n % 2
        block = wx.at[side, rows, spot(d, yy, side)]
        return pltpu.make_async_remote_copy(
            src_ref=block, dst_ref=block, send_sem=ws_sem.at[8 + n], recv_sem=wr_sem.at[8 + n],
            device_id=dev_sib, device_id_type=MESH)

    def pass_weights():
        for n in (0, 4, 1, 5, 2, 6, 3, 7):
            w_sends[n].wait_recv()
            w_copy(n, theirs).start()

    for load in loads:
        load.start()

    for d in range(1, SPAN):
        @pl.when(ctx < d)
        def _():
            kx[d, 0:ROWS, :] = jnp.zeros((ROWS, HD), jnp.bfloat16)
            kx[d, ROWS:, :] = jnp.full((SEGROWS, HD), -1.0, jnp.bfloat16)
            vv[d] = jnp.zeros((ROWS, HD), jnp.bfloat16)

    loads[0].wait()
    seg = seg_v[...].astype(jnp.float32)
    seg_lo, seg_hi = seg[:, :HD], seg[:, HD:]
    line = lax.broadcasted_iota(jnp.int32, (SEGROWS, HD), 0)
    both = jnp.where(line == 0, jnp.broadcast_to(seg_lo, (SEGROWS, HD)), jnp.broadcast_to(seg_hi, (SEGROWS, HD)))
    kx[0, ROWS:, :] = both.astype(jnp.bfloat16)
    first = jnp.min(seg, axis=1, keepdims=True)
    loads[1].wait()
    loads[2].wait()
    pl.semaphore_wait(barrier, 5 + core)

    def k_copy(index, slot, to_slot, device):
        return pltpu.make_async_remote_copy(
            src_ref=kx.at[slot], dst_ref=kx.at[to_slot],
            send_sem=ks_sem.at[index], recv_sem=kr_sem.at[to_slot],
            device_id=device, device_id_type=MESH)

    def v_copy(index, slot, to_slot, device):
        return pltpu.make_async_remote_copy(
            src_ref=vv.at[slot], dst_ref=vv.at[to_slot],
            send_sem=vs_sem.at[index], recv_sem=vr_sem.at[to_slot],
            device_id=device, device_id_type=MESH)

    plan = [
        (0, 2, dev_next, chip < chips - 1),
        (0, 1, dev_sib, core == 0),
        (2, 4, dev_next, (chip >= 1) & (chip < chips - 1)),
        (2, 3 - 2 * core, dev_sib, chip >= 1),
        (4, 5, (nxt * 2, head), (chip >= 2) & (chip < chips - 1) & (core == 1)),
        (4, 5 - 2 * core, dev_sib, chip >= 2),
    ]

    def send(make, slot, extra=True):
        for index, (source, target, device, cond) in enumerate(plan):
            if source == slot:
                @pl.when(cond & extra)
                def _():
                    make(index, source, target, device).start()

    def arrive(make, slot):
        @pl.when(ctx >= slot)
        def _():
            make(0, slot, slot, dev_next).wait_recv()

    send(k_copy, 0)
    send(v_copy, 0)
    for n in (0, 4, 1, 5, 2, 6, 3, 7):
        w_sends[n].start()
    loads[3].wait()

    scale = math.log2(math.e) / math.sqrt(HD)
    key_row = lax.broadcasted_iota(jnp.int32, (ROWS, ROWS), 0)
    count = share * (ROWS // LANES)
    peaks, totals = [None] * count, [None] * count

    def a_copy(side, n, rows, columns):
        return pltpu.make_async_remote_copy(
            src_ref=att.at[rows, columns], dst_ref=attx.at[side, rows, columns],
            send_sem=as_sem.at[side, n], recv_sem=ar_sem.at[side, n],
            device_id=partner[side][0], device_id_type=MESH)

    def a_copies(side, r):
        rows = pl.ds(*CHUNKS[r])
        if r == 0:
            return [a_copy(side, h, rows, pl.ds(h * HD, HD)) for h in range(share)]
        return [a_copy(side, share + r - 1, rows, pl.ds(0, share * HD))]

    def exchange(r):
        for side in range(2):
            for copy in a_copies(side, r):
                copy.start()

    tiles = [(h, half) for half in range(ROWS // LANES) for h in range(share)]

    def absorb(slot, allowed, place):
        last = place == SPAN - 1
        vt = None if last else vv[slot].T
        factors = [None] * len(tiles)
        for n, (h, half) in enumerate(tiles):
            cols = slice(half * LANES, (half + 1) * LANES)
            scores = lax.dot_general(
                kx[slot, 0:ROWS, :], q_v[cols, h * HD:(h + 1) * HD],
                (((1,), (1,)), ((), ())), preferred_element_type=jnp.float32)
            scores = jnp.where(allowed[:, cols], scores, NEG)
            top = jnp.max(scores, axis=0, keepdims=True)
            if place > 0:
                top = jnp.maximum(top, peaks[n])
            expo = jnp.exp2((scores - top) * scale)
            total = jnp.sum(expo, axis=0, keepdims=True)
            if place > 0:
                factors[n] = jnp.exp2((peaks[n] - top) * scale)
                total = total + totals[n] * factors[n]
            peaks[n], totals[n] = top, total
            if last:
                probs[n] = expo.astype(jnp.bfloat16)
                continue
            part = jnp.dot(vt, expo.astype(jnp.bfloat16), preferred_element_type=jnp.float32)
            if place > 0:
                part = part + acc[h, :, cols] * factors[n]
            acc[h, :, cols] = part
        if not last:
            return
        arrive(v_copy, slot)
        vt = vv[slot].T
        for n, (h, half) in enumerate(tiles):
            cols = slice(half * LANES, (half + 1) * LANES)
            part = jnp.dot(vt, probs[n], preferred_element_type=jnp.float32)
            part = (part + acc[h, :, cols] * factors[n]) / totals[n]
            att[cols, h * HD:(h + 1) * HD] = part.T.astype(jnp.bfloat16)
            if half == 0:
                for side in range(2):
                    a_copy(side, h, pl.ds(*CHUNKS[0]), pl.ds(h * HD, HD)).start()
                if h == share - 1:
                    exchange(1)

    seg_col = jnp.concatenate(
        [jnp.broadcast_to(seg_lo, (HD, HD)).T, jnp.broadcast_to(seg_hi, (HD, HD)).T], axis=0)
    seg_col = jnp.concatenate([seg_col, seg_col], axis=1)
    query_col = lax.broadcasted_iota(jnp.int32, (ROWS, ROWS), 1)
    absorb(0, (seg_col == seg) & (key_row <= query_col), 0)
    order = ((2 - core, core == 0), (1 + core, core == 1), (4 - core, core == 0), (3 + core, core == 1), (5, None))
    for place, (slot, passes) in enumerate(order):
        source = (2, 2, 4, 4, 5)[place]
        for make in (k_copy, v_copy) if place < SPAN - 2 else (k_copy,):
            arrive(make, slot)
            if passes is not None:
                send(make, source, passes)
        ids = kx[slot, ROWS:, :].astype(jnp.float32)
        same = jnp.where((line < 2) & (ids == first), 1.0, 0.0)
        count = jnp.sum(jnp.sum(same, axis=0, keepdims=True), axis=1, keepdims=True)
        start = jnp.where(seg == first, ROWS - count, float(ROWS)).astype(jnp.int32)
        absorb(slot, key_row >= start, place + 1)
        if place == 3:
            pl.when(chip % NZ < 2)(pass_weights)

    for load in loads[4:]:
        load.wait()
    pl.when(chip % NZ >= 2)(pass_weights)

    def s2_copy(side, r):
        rows = pl.ds(*CHUNKS[r])
        return pltpu.make_async_remote_copy(
            src_ref=s2.at[side, rows], dst_ref=r2.at[side, rows],
            send_sem=fs_sem.at[side, r], recv_sem=fr_sem.at[side, r],
            device_id=partner[1 - side][0], device_id_type=MESH)

    def s3_copy(r):
        rows = pl.ds(*CHUNKS[r])
        return pltpu.make_async_remote_copy(
            src_ref=s3.at[1 - yh, rows], dst_ref=r3.at[rows],
            send_sem=fs_sem.at[2, r], recv_sem=fr_sem.at[2, r],
            device_id=dev_y, device_id_type=MESH)

    def rows_of(r):
        return slice(CHUNKS[r][0], CHUNKS[r][0] + CHUNKS[r][1])

    def own_part():
        for side in range(2):
            own[side] = jnp.dot(att[...], wx[side, 0:depth], preferred_element_type=jnp.float32)

    def both_parts(r):
        for side in range(2):
            for copy in a_copies(side, r):
                copy.wait_recv()
            if r == 0:
                for n in range(side * 4, side * 4 + 4):
                    w_copy(n, others).wait_recv()
            both = own[side, rows_of(r)] + jnp.dot(
                attx[side, rows_of(r)], wx[side, depth:], preferred_element_type=jnp.float32)
            s2[side, rows_of(r)] = both[:, BLOCK:].astype(jnp.bfloat16)
            s2_copy(side, r).start()
            own[side, rows_of(r), 0:BLOCK] = both[:, :BLOCK]

    def hand_on(r):
        for side in range(2):
            s2_copy(side, r).wait_recv()
            both = own[side, rows_of(r), 0:BLOCK] + r2[side, rows_of(r)].astype(jnp.float32)
            for yy in range(2):
                first, width, place = PARTS[side][yy]
                res[yy, rows_of(r), first:first + width] = both[:, place:place + width]
                s3[yy, rows_of(r), first:first + width] = both[:, place:place + width].astype(jnp.bfloat16)
        s3_copy(r).start()

    own_part()
    for r in range(NCH):
        both_parts(r)
        if r + 2 < NCH:
            exchange(r + 2)
        if r >= 1:
            hand_on(r - 1)
    hand_on(NCH - 1)

    for r in range(NCH):
        s3_copy(r).wait_recv()
        out[rows_of(r)] = (res[yh, rows_of(r)] + r3[rows_of(r)].astype(jnp.float32)).astype(jnp.bfloat16)
    for r in range(NCH):
        s3_copy(r).wait_send()
        for side in range(2):
            s2_copy(side, r).wait_send()
            for copy in a_copies(side, r):
                copy.wait_send()
    for copy in w_sends:
        copy.wait_send()
    for n in range(8):
        w_copy(n, theirs).wait_send()
    for make in (k_copy, v_copy):
        for index, (source, target, device, cond) in enumerate(plan):
            @pl.when(cond)
            def _():
                make(index, source, target, device).wait_send()


def solution(mesh):
    chips = mesh.shape["ctx"] // 2

    def shards(queries, keys, values, segment_ids, out_weight):
        share = queries.shape[1] // HD
        cols = out_weight.shape[1] // mesh.shape["head"]
        bf, f32 = jnp.bfloat16, jnp.float32
        depth = out_weight.shape[0]
        return pl.pallas_call(
            functools.partial(kernel, chips, share),
            name="attend_project",
            out_shape=pltpu.VMEM((ROWS, cols), bf),
            in_specs=[pl.BlockSpec(memory_space=pl.ANY)] * 5,
            out_specs=pl.BlockSpec(memory_space=pltpu.VMEM),
            scratch_shapes=[
                pltpu.VMEM(queries.shape, bf),
                pltpu.VMEM((SPAN, ROWS + SEGROWS, HD), bf),
                pltpu.VMEM((SPAN, ROWS, HD), bf),
                pltpu.VMEM((1, ROWS), jnp.int32),
                pltpu.VMEM((2, 2 * depth, 2 * BLOCK), bf),
                pltpu.VMEM((share, HD, ROWS), f32),
                pltpu.VMEM((share * (ROWS // LANES), ROWS, LANES), bf),
                pltpu.VMEM(queries.shape, bf),
                pltpu.VMEM((2, *queries.shape), bf),
                pltpu.VMEM((2, ROWS, 2 * BLOCK), f32),
                pltpu.VMEM((2, ROWS, BLOCK), bf),
                pltpu.VMEM((2, ROWS, BLOCK), bf),
                pltpu.VMEM((2, ROWS, BLOCK), f32),
                pltpu.VMEM((2, ROWS, BLOCK), bf),
                pltpu.VMEM((ROWS, BLOCK), bf),
                pltpu.SemaphoreType.DMA((12,)),
                pltpu.SemaphoreType.DMA((SPAN,)),
                pltpu.SemaphoreType.DMA((SPAN,)),
                pltpu.SemaphoreType.DMA((SPAN,)),
                pltpu.SemaphoreType.DMA((SPAN,)),
                pltpu.SemaphoreType.DMA((16,)),
                pltpu.SemaphoreType.DMA((16,)),
                pltpu.SemaphoreType.DMA((2, share + NCH - 1)),
                pltpu.SemaphoreType.DMA((2, share + NCH - 1)),
                pltpu.SemaphoreType.DMA((3, NCH)),
                pltpu.SemaphoreType.DMA((3, NCH)),
            ],
            compiler_params=pltpu.CompilerParams(
                collective_id=0, has_side_effects=True, vmem_limit_bytes=60 * 2**20),
        )(queries, keys, values, segment_ids.reshape(1, ROWS), out_weight)

    in_specs = (P("ctx", "head"), P("ctx", "head"), P("ctx", "head"), P("ctx"), P("head", None))
    return jax.shard_map(shards, mesh=mesh, in_specs=in_specs, out_specs=P("ctx", "head"), check_vma=False)
```

```python
import functools
import math

import jax
import jax.numpy as jnp
from jax import lax
from jax.experimental import pallas as pl
from jax.experimental.pallas import tpu as pltpu
from jax.sharding import PartitionSpec as P

HD = 128
SPAN = 6
ROWS = 256
SEGROWS = 16
NX = 4
NZ = 12
BLOCK = 640
PARTS = (((0, 384, 0), (0, 256, 384)), ((384, 256, 0), (256, 384, 256)))
CHUNKS = ((0, 64), (64, 64), (128, 64), (192, 64))
NCH = len(CHUNKS)
MESH = pl.DeviceIdType.MESH
NEG = -1e30
LANES = 128


def kernel(
    chips, share,
    q_hbm, k_hbm, v_hbm, s_hbm, w_hbm, out,
    q_v, kx, vv, seg_v, wx, acc, probs, att, attx, own, s2, r2, res, s3, r3,
    load_sem, ks_sem, kr_sem, vs_sem, vr_sem, ws_sem, wr_sem, as_sem, ar_sem, fs_sem, fr_sem,
):
    ctx = lax.axis_index("ctx")
    head = lax.axis_index("head")
    chip, core = ctx // 2, ctx % 2
    yh, x = head // NX, head % NX
    x1 = x + 1 - 2 * (x % 2)
    x3 = NX - 1 - x
    xo = (x + 2) % NX
    nxt, prv = (chip + 1) % chips, (chip + chips - 1) % chips
    dev_x1 = (ctx, yh * NX + x1)
    dev_x3 = (ctx, yh * NX + x3)
    dev_y = (ctx, (1 - yh) * NX + x)
    dev_sib = (chip * 2 + 1 - core, head)
    dev_next = (nxt * 2 + core, head)

    barrier = pltpu.get_barrier_semaphore()
    for device in (dev_y, dev_x1, dev_x3, dev_sib, (prv * 2 + core, head)):
        pl.semaphore_signal(barrier, inc=1, device_id=device, device_id_type=MESH)

    @pl.when(core == 0)
    def _():
        pl.semaphore_signal(barrier, inc=1, device_id=(prv * 2 + 1, head), device_id_type=MESH)

    depth = w_hbm.shape[0]
    dests = ((x, x3), (x, x1))
    partner = ((dev_x1, x1, xo), (dev_x3, x3, xo))

    def span(xx, yy, side):
        first, width, _ = PARTS[side][yy]
        return pl.ds(pl.multiple_of((yy * NX + xx) * BLOCK + first, HD), width)

    def spot(d, yy, side):
        return pl.ds(d * BLOCK + PARTS[side][yy][2], PARTS[side][yy][1])

    part = depth // 2
    mine = pl.ds(pl.multiple_of(core * part, 16), part)
    theirs = pl.ds(pl.multiple_of(depth + core * part, 16), part)
    others = pl.ds(pl.multiple_of(depth + (1 - core) * part, 16), part)
    loads = [
        pltpu.make_async_copy(s_hbm, seg_v, load_sem.at[0]),
        pltpu.make_async_copy(k_hbm, kx.at[0, pl.ds(0, ROWS)], load_sem.at[1]),
        pltpu.make_async_copy(v_hbm, vv.at[0], load_sem.at[2]),
        pltpu.make_async_copy(q_hbm, q_v, load_sem.at[3]),
    ]
    w_sends = []
    for side in range(2):
        for d in range(2):
            for yy in range(2):
                n = (side * 2 + d) * 2 + yy
                loads.append(pltpu.make_async_copy(
                    w_hbm.at[:, span(dests[side][d], yy, side)],
                    wx.at[side, pl.ds(0, depth), spot(d, yy, side)], load_sem.at[4 + n]))
                device, *columns = partner[side]
                w_sends.append(pltpu.make_async_remote_copy(
                    src_ref=w_hbm.at[mine, span(columns[d], yy, side)],
                    dst_ref=wx.at[side, theirs, spot(d, yy, side)],
                    send_sem=ws_sem.at[n], recv_sem=wr_sem.at[n],
                    device_id=device, device_id_type=MESH))

    def w_copy(n, rows):
        side, d, yy = n // 4, n // 2 % 2, n % 2
        block = wx.at[side, rows, spot(d, yy, side)]
        return pltpu.make_async_remote_copy(
            src_ref=block, dst_ref=block, send_sem=ws_sem.at[8 + n], recv_sem=wr_sem.at[8 + n],
            device_id=dev_sib, device_id_type=MESH)

    def pass_weights():
        for n in (0, 4, 1, 5, 2, 6, 3, 7):
            w_sends[n].wait_recv()
            w_copy(n, theirs).start()

    for load in loads:
        load.start()

    for d in range(1, SPAN):
        @pl.when(ctx < d)
        def _():
            kx[d, 0:ROWS, :] = jnp.zeros((ROWS, HD), jnp.bfloat16)
            kx[d, ROWS:, :] = jnp.full((SEGROWS, HD), -1.0, jnp.bfloat16)
            vv[d] = jnp.zeros((ROWS, HD), jnp.bfloat16)

    loads[0].wait()
    seg = seg_v[...].astype(jnp.float32)
    seg_lo, seg_hi = seg[:, :HD], seg[:, HD:]
    line = lax.broadcasted_iota(jnp.int32, (SEGROWS, HD), 0)
    both = jnp.where(line == 0, jnp.broadcast_to(seg_lo, (SEGROWS, HD)), jnp.broadcast_to(seg_hi, (SEGROWS, HD)))
    kx[0, ROWS:, :] = both.astype(jnp.bfloat16)
    first = jnp.min(seg, axis=1, keepdims=True)
    loads[1].wait()
    loads[2].wait()
    pl.semaphore_wait(barrier, 5 + core)

    def k_copy(index, slot, to_slot, device):
        return pltpu.make_async_remote_copy(
            src_ref=kx.at[slot], dst_ref=kx.at[to_slot],
            send_sem=ks_sem.at[index], recv_sem=kr_sem.at[to_slot],
            device_id=device, device_id_type=MESH)

    def v_copy(index, slot, to_slot, device):
        return pltpu.make_async_remote_copy(
            src_ref=vv.at[slot], dst_ref=vv.at[to_slot],
            send_sem=vs_sem.at[index], recv_sem=vr_sem.at[to_slot],
            device_id=device, device_id_type=MESH)

    plan = [
        (0, 2, dev_next, chip < chips - 1),
        (0, 1, dev_sib, core == 0),
        (2, 4, dev_next, (chip >= 1) & (chip < chips - 1)),
        (2, 3 - 2 * core, dev_sib, chip >= 1),
        (4, 5, (nxt * 2, head), (chip >= 2) & (chip < chips - 1) & (core == 1)),
        (4, 5 - 2 * core, dev_sib, chip >= 2),
    ]

    def send(make, slot, extra=True):
        for index, (source, target, device, cond) in enumerate(plan):
            if source == slot:
                @pl.when(cond & extra)
                def _():
                    make(index, source, target, device).start()

    def arrive(make, slot):
        @pl.when(ctx >= slot)
        def _():
            make(0, slot, slot, dev_next).wait_recv()

    send(k_copy, 0)
    send(v_copy, 0)
    def send_weights():
        for n in (0, 4, 1, 5, 2, 6, 3, 7):
            w_sends[n].start()

    pl.when(chip % NZ < 9)(send_weights)
    loads[3].wait()

    scale = math.log2(math.e) / math.sqrt(HD)
    key_row = lax.broadcasted_iota(jnp.int32, (ROWS, ROWS), 0)
    count = share * (ROWS // LANES)
    peaks, totals = [None] * count, [None] * count

    def a_copy(side, n, rows, columns):
        return pltpu.make_async_remote_copy(
            src_ref=att.at[rows, columns], dst_ref=attx.at[side, rows, columns],
            send_sem=as_sem.at[side, n], recv_sem=ar_sem.at[side, n],
            device_id=partner[side][0], device_id_type=MESH)

    def a_copies(side, r):
        rows = pl.ds(*CHUNKS[r])
        if r == 0:
            return [a_copy(side, h, rows, pl.ds(h * HD, HD)) for h in range(share)]
        return [a_copy(side, share + r - 1, rows, pl.ds(0, share * HD))]

    def exchange(r):
        for side in range(2):
            for copy in a_copies(side, r):
                copy.start()

    tiles = [(h, half) for half in range(ROWS // LANES) for h in range(share)]

    def absorb(slot, allowed, place):
        last = place == SPAN - 1
        vt = None if last else vv[slot].T
        factors = [None] * len(tiles)
        for n, (h, half) in enumerate(tiles):
            cols = slice(half * LANES, (half + 1) * LANES)
            scores = lax.dot_general(
                kx[slot, 0:ROWS, :], q_v[cols, h * HD:(h + 1) * HD],
                (((1,), (1,)), ((), ())), preferred_element_type=jnp.float32)
            scores = jnp.where(allowed[:, cols], scores, NEG)
            top = jnp.max(scores, axis=0, keepdims=True)
            if place > 0:
                top = jnp.maximum(top, peaks[n])
            expo = jnp.exp2((scores - top) * scale)
            total = jnp.sum(expo, axis=0, keepdims=True)
            if place > 0:
                factors[n] = jnp.exp2((peaks[n] - top) * scale)
                total = total + totals[n] * factors[n]
            peaks[n], totals[n] = top, total
            if last:
                probs[n] = expo.astype(jnp.bfloat16)
                continue
            part = jnp.dot(vt, expo.astype(jnp.bfloat16), preferred_element_type=jnp.float32)
            if place > 0:
                part = part + acc[h, :, cols] * factors[n]
            acc[h, :, cols] = part
        if not last:
            return
        arrive(v_copy, slot)
        vt = vv[slot].T
        for n, (h, half) in enumerate(tiles):
            cols = slice(half * LANES, (half + 1) * LANES)
            part = jnp.dot(vt, probs[n], preferred_element_type=jnp.float32)
            part = (part + acc[h, :, cols] * factors[n]) / totals[n]
            att[cols, h * HD:(h + 1) * HD] = part.T.astype(jnp.bfloat16)
            if half == 0:
                for side in range(2):
                    a_copy(side, h, pl.ds(*CHUNKS[0]), pl.ds(h * HD, HD)).start()
                if h == share - 1:
                    exchange(1)

    seg_col = jnp.concatenate(
        [jnp.broadcast_to(seg_lo, (HD, HD)).T, jnp.broadcast_to(seg_hi, (HD, HD)).T], axis=0)
    seg_col = jnp.concatenate([seg_col, seg_col], axis=1)
    query_col = lax.broadcasted_iota(jnp.int32, (ROWS, ROWS), 1)
    absorb(0, (seg_col == seg) & (key_row <= query_col), 0)
    order = ((2 - core, core == 0), (1 + core, core == 1), (4 - core, core == 0), (3 + core, core == 1), (5, None))
    for place, (slot, passes) in enumerate(order):
        source = (2, 2, 4, 4, 5)[place]
        for make in (k_copy, v_copy) if place < SPAN - 2 else (k_copy,):
            arrive(make, slot)
            if passes is not None:
                send(make, source, passes)
        ids = kx[slot, ROWS:, :].astype(jnp.float32)
        same = jnp.where((line < 2) & (ids == first), 1.0, 0.0)
        count = jnp.sum(jnp.sum(same, axis=0, keepdims=True), axis=1, keepdims=True)
        start = jnp.where(seg == first, ROWS - count, float(ROWS)).astype(jnp.int32)
        absorb(slot, key_row >= start, place + 1)
        if place == 1:
            pl.when(chip % NZ >= 9)(send_weights)
        if place == 3:
            pl.when(chip % NZ < 2)(pass_weights)

    for load in loads[4:]:
        load.wait()
    pl.when(chip % NZ >= 2)(pass_weights)

    def s2_copy(side, r):
        rows = pl.ds(*CHUNKS[r])
        return pltpu.make_async_remote_copy(
            src_ref=s2.at[side, rows], dst_ref=r2.at[side, rows],
            send_sem=fs_sem.at[side, r], recv_sem=fr_sem.at[side, r],
            device_id=partner[1 - side][0], device_id_type=MESH)

    def s3_copy(r):
        rows = pl.ds(*CHUNKS[r])
        return pltpu.make_async_remote_copy(
            src_ref=s3.at[1 - yh, rows], dst_ref=r3.at[rows],
            send_sem=fs_sem.at[2, r], recv_sem=fr_sem.at[2, r],
            device_id=dev_y, device_id_type=MESH)

    def rows_of(r):
        return slice(CHUNKS[r][0], CHUNKS[r][0] + CHUNKS[r][1])

    def own_part():
        for side in range(2):
            own[side] = jnp.dot(att[...], wx[side, 0:depth], preferred_element_type=jnp.float32)

    def both_parts(r):
        for side in range(2):
            for copy in a_copies(side, r):
                copy.wait_recv()
            if r == 0:
                for n in range(side * 4, side * 4 + 4):
                    w_copy(n, others).wait_recv()
            both = own[side, rows_of(r)] + jnp.dot(
                attx[side, rows_of(r)], wx[side, depth:], preferred_element_type=jnp.float32)
            s2[side, rows_of(r)] = both[:, BLOCK:].astype(jnp.bfloat16)
            s2_copy(side, r).start()
            own[side, rows_of(r), 0:BLOCK] = both[:, :BLOCK]

    def hand_on(r):
        for side in range(2):
            s2_copy(side, r).wait_recv()
            both = own[side, rows_of(r), 0:BLOCK] + r2[side, rows_of(r)].astype(jnp.float32)
            for yy in range(2):
                first, width, place = PARTS[side][yy]
                res[yy, rows_of(r), first:first + width] = both[:, place:place + width]
                s3[yy, rows_of(r), first:first + width] = both[:, place:place + width].astype(jnp.bfloat16)
        s3_copy(r).start()

    own_part()
    for r in range(NCH):
        both_parts(r)
        if r + 2 < NCH:
            exchange(r + 2)
        if r >= 1:
            hand_on(r - 1)
    hand_on(NCH - 1)

    for r in range(NCH):
        s3_copy(r).wait_recv()
        out[rows_of(r)] = (res[yh, rows_of(r)] + r3[rows_of(r)].astype(jnp.float32)).astype(jnp.bfloat16)
    for r in range(NCH):
        s3_copy(r).wait_send()
        for side in range(2):
            s2_copy(side, r).wait_send()
            for copy in a_copies(side, r):
                copy.wait_send()
    for copy in w_sends:
        copy.wait_send()
    for n in range(8):
        w_copy(n, theirs).wait_send()
    for make in (k_copy, v_copy):
        for index, (source, target, device, cond) in enumerate(plan):
            @pl.when(cond)
            def _():
                make(index, source, target, device).wait_send()


def solution(mesh):
    chips = mesh.shape["ctx"] // 2

    def shards(queries, keys, values, segment_ids, out_weight):
        share = queries.shape[1] // HD
        cols = out_weight.shape[1] // mesh.shape["head"]
        bf, f32 = jnp.bfloat16, jnp.float32
        depth = out_weight.shape[0]
        return pl.pallas_call(
            functools.partial(kernel, chips, share),
            name="attend_project",
            out_shape=pltpu.VMEM((ROWS, cols), bf),
            in_specs=[pl.BlockSpec(memory_space=pl.ANY)] * 5,
            out_specs=pl.BlockSpec(memory_space=pltpu.VMEM),
            scratch_shapes=[
                pltpu.VMEM(queries.shape, bf),
                pltpu.VMEM((SPAN, ROWS + SEGROWS, HD), bf),
                pltpu.VMEM((SPAN, ROWS, HD), bf),
                pltpu.VMEM((1, ROWS), jnp.int32),
                pltpu.VMEM((2, 2 * depth, 2 * BLOCK), bf),
                pltpu.VMEM((share, HD, ROWS), f32),
                pltpu.VMEM((share * (ROWS // LANES), ROWS, LANES), bf),
                pltpu.VMEM(queries.shape, bf),
                pltpu.VMEM((2, *queries.shape), bf),
                pltpu.VMEM((2, ROWS, 2 * BLOCK), f32),
                pltpu.VMEM((2, ROWS, BLOCK), bf),
                pltpu.VMEM((2, ROWS, BLOCK), bf),
                pltpu.VMEM((2, ROWS, BLOCK), f32),
                pltpu.VMEM((2, ROWS, BLOCK), bf),
                pltpu.VMEM((ROWS, BLOCK), bf),
                pltpu.SemaphoreType.DMA((12,)),
                pltpu.SemaphoreType.DMA((SPAN,)),
                pltpu.SemaphoreType.DMA((SPAN,)),
                pltpu.SemaphoreType.DMA((SPAN,)),
                pltpu.SemaphoreType.DMA((SPAN,)),
                pltpu.SemaphoreType.DMA((16,)),
                pltpu.SemaphoreType.DMA((16,)),
                pltpu.SemaphoreType.DMA((2, share + NCH - 1)),
                pltpu.SemaphoreType.DMA((2, share + NCH - 1)),
                pltpu.SemaphoreType.DMA((3, NCH)),
                pltpu.SemaphoreType.DMA((3, NCH)),
            ],
            compiler_params=pltpu.CompilerParams(
                collective_id=0, has_side_effects=True, vmem_limit_bytes=60 * 2**20),
        )(queries, keys, values, segment_ids.reshape(1, ROWS), out_weight)

    in_specs = (P("ctx", "head"), P("ctx", "head"), P("ctx", "head"), P("ctx"), P("head", None))
    return jax.shard_map(shards, mesh=mesh, in_specs=in_specs, out_specs=P("ctx", "head"), check_vma=False)
```
